512 devices in a mesh: blk: 16 (over y, core), pair: 16 (over z, x_hi), seq: 2 (over x_lo).
Axes of the slice: x: 4 (x_hi: 2, x_lo: 2; x = x_hi * 2 + x_lo), y: 8, z: 8, core: 2. Of those that a mesh axis runs over, the one named last changes fastest.
Arguments:
- resp_x: bfloat16 [16, 16, 256, 5120], P('blk', 'pair', 'seq'), may hold values from -6 to 6
- queries: bfloat16 [16, 16, 256, 2560], P('blk', 'pair', 'seq'), may hold values from -5 to 5
- key_weight: bfloat16 [5120, 512], P('blk'), may hold values from -0.078125 to 0.078125
- value_weight: bfloat16 [5120, 512], P('blk'), may hold values from -0.078125 to 0.078125
- prompt_key: bfloat16 [16, 2048, 512], P('blk', ('pair', 'seq')), may hold values from -5 to 5
- cached_prompt_values: bfloat16 [16, 2048, 512], P('blk', ('pair', 'seq')), may hold values from -6 to 6
- lengths: int32 [16, 16], P('blk', 'pair'), may hold values from 1 to 256, as said below
- prompt_len: int32 [16], P('blk'), may hold values from 1024 to 2048, as said below
Outputs:
- context: bfloat16 [16, 16, 256, 2560], P('blk', 'pair', 'seq')
The draws below stay inside these ranges and needn't reach their ends.
Inputs may be any that keep to these rules, and one draw needn't show every extreme that they name: `lengths`: every response has at least one live position; some response of the batch has all 256 positions live. `prompt_len`: at least half of each prompt's cached positions are live; some prompt has all 2048 live.
All inputs are finite; a program needn't handle non-finite values.
Results may differ from the reference program's by a relative error of at most 0.0085.
Values may be sent and summed in bfloat16 or wider, within the bound.
A program may use at most 128 MiB of HBM per device.

```python
import jax
import jax.numpy as jnp
from jax import lax

MODEL_WIDTH = 5120
QUERY_HEADS = 20
KEY_VALUE_HEADS = 4
HEAD_SIZE = 128
RESPONSE_LENGTH = 256
PROMPT_POSITIONS = 2048
N_BLK = 16
N_PAIR = 16


def draw_queries(key, part):
    key = jax.random.fold_in(key, 21)
    array_shape = (N_BLK, N_PAIR, RESPONSE_LENGTH, QUERY_HEADS * HEAD_SIZE)
    value_matrix = jnp.clip(jax.random.normal(key, array_shape, jnp.float32), -4.0, 4.0)
    return value_matrix.astype(jnp.bfloat16)


def draw_prompt_key(key, part):
    key = jax.random.fold_in(key, 31)
    array_shape = (N_BLK, PROMPT_POSITIONS, KEY_VALUE_HEADS * HEAD_SIZE)
    value_matrix = jnp.clip(jax.random.normal(key, array_shape, jnp.float32), -4.0, 4.0)
    return value_matrix.astype(jnp.bfloat16)


def draw_lengths(key, part):
    key = jax.random.fold_in(key, 41)
    value_matrix = jax.random.randint(key, (N_BLK * N_PAIR,), 1, RESPONSE_LENGTH + 1)
    spot = jax.random.randint(jax.random.fold_in(key, 1), (), 0, N_BLK * N_PAIR)
    value_matrix = jnp.where(jnp.arange(N_BLK * N_PAIR) == spot, RESPONSE_LENGTH, value_matrix)
    return value_matrix.reshape(N_BLK, N_PAIR).astype(jnp.int32)


def draw_prompt_len(key, part):
    key = jax.random.fold_in(key, 51)
    value_matrix = jax.random.randint(key, (N_BLK,), PROMPT_POSITIONS // 2, PROMPT_POSITIONS + 1)
    spot = jax.random.randint(jax.random.fold_in(key, 1), (), 0, N_BLK)
    value_matrix = jnp.where(jnp.arange(N_BLK) == spot, PROMPT_POSITIONS, value_matrix)
    return value_matrix.astype(jnp.int32)


def steps_of(key, dims, pieces, smallest, top_value):
    factor_of = 1.0
    for dim, parts in pieces:
        draws = jax.random.uniform(jax.random.fold_in(jax.random.fold_in(key, 6), dim), (parts,), jnp.float32, smallest / len(pieces), top_value / len(pieces))
        factor_of = factor_of * jnp.repeat(jnp.exp(draws), dims[dim] // parts).reshape((-1,) + (1,) * (len(dims) - 1 - dim))
    return factor_of


def centred(own_key, shape, deviation, most, cuts=(), kind=jnp.bfloat16):
    drawn = deviation * jax.random.normal(own_key, shape, jnp.float32)
    if cuts:
        drawn = drawn * steps_of(own_key, shape, cuts, -0.22, 0.18)
    return jnp.clip(drawn, -most, most).astype(kind)


def setup_inputs(seed: int = 0) -> dict:
    splits = jax.random.split(jax.random.key(seed), 9)
    resp_x = centred(splits[0], (N_BLK, N_PAIR, RESPONSE_LENGTH, MODEL_WIDTH), 1.0, 6.0, ((0, 16), (1, 16), (2, 2)))
    queries = draw_queries(jax.random.fold_in(splits[8], 71), 0)
    key_weight = centred(splits[2], (MODEL_WIDTH, KEY_VALUE_HEADS * HEAD_SIZE), MODEL_WIDTH ** -0.5, 0.078125, ((0, 16),))
    value_weight = centred(splits[3], (MODEL_WIDTH, KEY_VALUE_HEADS * HEAD_SIZE), MODEL_WIDTH ** -0.5, 0.078125, ((0, 16),))
    prompt_key = draw_prompt_key(jax.random.fold_in(splits[8], 71), 0)
    cached_prompt_values = centred(splits[5], (N_BLK, PROMPT_POSITIONS, KEY_VALUE_HEADS * HEAD_SIZE), 1.0, 6.0, ((0, 16), (1, 32)))
    lengths = draw_lengths(jax.random.fold_in(splits[8], 71), 0)
    prompt_len = draw_prompt_len(jax.random.fold_in(splits[8], 71), 0)
    return dict(resp_x=resp_x, queries=queries, key_weight=key_weight, value_weight=value_weight, prompt_key=prompt_key, cached_prompt_values=cached_prompt_values, lengths=lengths, prompt_len=prompt_len)


NEGATIVE_FILL = -1e30


def one_response(resp_rows, query_matrix, length, pkey, pval, plen, key_weight, value_weight):
    new_key = jnp.dot(resp_rows, key_weight, preferred_element_type=jnp.float32).astype(jnp.bfloat16)
    new_value = jnp.dot(resp_rows, value_weight, preferred_element_type=jnp.float32).astype(jnp.bfloat16)
    key_matrix = jnp.concatenate([pkey, new_key], 0).astype(jnp.float32)
    value_matrix = jnp.concatenate([pval, new_value], 0).astype(jnp.float32)
    total_sum = key_matrix.shape[0]
    head_group = QUERY_HEADS // KEY_VALUE_HEADS
    query_head_rows = query_matrix.astype(jnp.float32).reshape(RESPONSE_LENGTH, KEY_VALUE_HEADS, head_group, HEAD_SIZE)
    key_head_rows = key_matrix.reshape(total_sum, KEY_VALUE_HEADS, HEAD_SIZE)
    value_head_rows = value_matrix.reshape(total_sum, KEY_VALUE_HEADS, HEAD_SIZE)
    scores = jnp.einsum("rhgd,khd->hgrk", query_head_rows, key_head_rows) * (HEAD_SIZE ** -0.5)
    positions = jnp.arange(RESPONSE_LENGTH, dtype=jnp.int32)[:, None]
    columns = jnp.arange(total_sum, dtype=jnp.int32)[None, :]
    allowed = jnp.where(columns < PROMPT_POSITIONS, columns < plen, columns - PROMPT_POSITIONS <= positions)
    scores = jnp.where(allowed, scores, NEGATIVE_FILL)
    top = jnp.max(scores, axis=-1, keepdims=True)
    weight = jnp.where(allowed, jnp.exp(scores - top), 0.0)
    denom = jnp.sum(weight, axis=-1)
    rounded = lax.optimization_barrier(weight.astype(jnp.bfloat16)).astype(jnp.float32)
    mixed_rows = jnp.einsum("hgrk,khd->rhgd", rounded, value_head_rows)
    mixed_rows = mixed_rows / jnp.transpose(denom, (2, 0, 1))[..., None]
    live = jnp.arange(RESPONSE_LENGTH, dtype=jnp.int32)[:, None] < length
    return jnp.where(live, mixed_rows.reshape(RESPONSE_LENGTH, QUERY_HEADS * HEAD_SIZE), 0.0).astype(jnp.bfloat16)


def reference(resp_x, queries, key_weight, value_weight, prompt_key, cached_prompt_values, lengths, prompt_len):
    def per_prompt(items):
        resp_group, query_group, length_group, pkey, pval, plen = items

        def per_response(inner):
            resp_rows, query_matrix, length = inner
            return one_response(resp_rows, query_matrix, length, pkey, pval, plen, key_weight, value_weight)

        return lax.map(per_response, (resp_group, query_group, length_group))

    return lax.map(per_prompt, (resp_x, queries, lengths, prompt_key, cached_prompt_values, prompt_len))
```

```python
import functools
import math

import jax
import jax.numpy as jnp
from jax import lax
from jax.experimental import pallas as pl
from jax.experimental.pallas import tpu as pltpu
from jax.sharding import PartitionSpec as P

KV_HEADS = 4
HEAD = 128
GROUP = 5
NY, NZ, NX = 8, 8, 4
ROWS = 128
SHARD = 64
BLOCK = NX * SHARD
WROWS = 320
XCOLS = 2 * WROWS
GCOLS = 256
QROWS = GROUP * ROWS
NEG = -1e30
SCALE = HEAD ** (-0.5) * math.log2(math.e)
MESH = pl.DeviceIdType.MESH
F32 = jnp.float32
BF16 = jnp.bfloat16
U = 3.3
W = 4.0
ZS = 5.0


def kernel(
    x_ref, q_ref, kw_ref, vw_ref, pk_ref, pv_ref, plen_ref, o_ref,
    kvbuf, wbuf, xbuf, qs, pacc, psend, precv, newkv, top_ref, den_ref, acc_ref,
    own_sem, q_sem, xl_sem, wl_sem,
    ph_s, ph_r, zs_s, zs_r, h_s, h_r, y_s, y_r, b_s, b_r, x_s, x_r, p_s, p_r,
):
    blk, pair, s = lax.axis_index("blk"), lax.axis_index("pair"), lax.axis_index("seq")
    y, c = blk // 2, blk % 2
    z, hi = pair // 2, pair % 2
    x = hi * 2 + s
    q = (y + s) % 2

    def y_dev(step):
        return {"blk": ((y + step + NY) % NY) * 2 + c, "pair": pair, "seq": s}

    def z_dev(step):
        return {"blk": blk, "pair": ((z + step + NZ) % NZ) * 2 + hi, "seq": s}

    sib = {"blk": y * 2 + (1 - c), "pair": pair, "seq": s}
    sx = {"blk": blk, "pair": pair, "seq": 1 - s}
    hx = {"blk": blk, "pair": z * 2 + (1 - hi), "seq": 1 - s}
    x2 = {"blk": blk, "pair": z * 2 + (1 - hi), "seq": s}
    x_peers = (sx, hx, x2)
    peer_x = (hi * 2 + 1 - s, 3 - x, (1 - hi) * 2 + s)

    def remote(src, dst, ss, rs, dev):
        return pltpu.make_async_remote_copy(
            src_ref=src, dst_ref=dst, send_sem=ss, recv_sem=rs, device_id=dev, device_id_type=MESH
        )

    sends = []

    local_q = [
        pltpu.make_async_copy(
            q_ref.at[0, 0, :, pl.ds((h * GROUP + g) * HEAD, HEAD)],
            qs.at[h, pl.ds(g * ROWS, ROWS)],
            q_sem.at[h * GROUP + g],
        )
        for h in range(KV_HEADS)
        for g in range(GROUP)
    ]
    cached = (pk_ref, pv_ref)
    own_rows = pl.ds(pl.multiple_of(x * SHARD, SHARD), SHARD)
    local_kv = [
        pltpu.make_async_copy(cached[i].at[0], kvbuf.at[i, z, own_rows], own_sem.at[i]) for i in range(2)
    ]
    own_x_rows = pl.ds(pl.multiple_of(s * ROWS, ROWS), ROWS)

    def x_cols(t, parity):
        return pl.ds(pl.multiple_of((2 * t + parity) * XCOLS, HEAD), XCOLS)

    local_x = [
        pltpu.make_async_copy(x_ref.at[0, 0, :, x_cols(t, s)], xbuf.at[t, own_x_rows], xl_sem.at[t])
        for t in range(4)
    ]
    weights = (kw_ref, vw_ref)

    def own_w(g):
        return weights[g // 2].at[:, pl.ds((g % 2) * GCOLS, GCOLS)]

    w_rows = pl.ds(pl.multiple_of(c * WROWS, 64), WROWS)
    w_other = pl.ds(pl.multiple_of((1 - c) * WROWS, 64), WROWS)
    local_w = [
        pltpu.make_async_copy(own_w(g), wbuf.at[g, y // 2, w_rows], wl_sem.at[g]) for g in range(4)
    ]
    for copy in local_kv + local_q + local_x:
        copy.start()

    @pl.when(q == 0)
    def _():
        for copy in local_w:
            copy.start()

    barrier = pltpu.get_barrier_semaphore()
    for dev in (sib, sx, hx, x2, y_dev(1), y_dev(-1), z_dev(1), z_dev(-1)):
        pl.semaphore_signal(barrier, inc=1, device_id=dev, device_id_type=MESH)
    pl.semaphore_wait(barrier, 8)

    phase = []
    for p in (2, 0, 1):
        for i in range(2):
            copy = remote(cached[i].at[0], kvbuf.at[i, z, own_rows], ph_s.at[i, p], ph_r.at[i, p], x_peers[p])
            copy.start()
            phase.append((i, p, copy))

    REACH = {(0, 0): 4, (0, 1): 3, (1, 0): 3, (1, 1): 4}

    def reach(way, g):
        return REACH[(way, g % 2)]

    def y_step(way):
        return 1 if way == 0 else -1

    def y_from(way, d):
        return (y - d + NY) % NY if way == 0 else (y + d) % NY

    def y_send(way, g, d, src):
        t = y_from(way, d) // 2
        return remote(
            src, wbuf.at[g, t, w_rows], y_s.at[way, g, d], y_r.at[way, g, d + 1], y_dev(y_step(way))
        )

    def y_recv(way, g, d):
        t = y_from(way, d) // 2
        ref = wbuf.at[g, t, w_rows]
        return remote(ref, ref, y_s.at[way, g, d], y_r.at[way, g, d], y_dev(-y_step(way)))

    def sib_send(g, t, src):
        return remote(src, wbuf.at[g, t, w_rows], b_s.at[g, t], b_r.at[g, t], sib)

    def sib_recv(g, t):
        ref = wbuf.at[g, t, w_other]
        return remote(ref, ref, b_s.at[g, t], b_r.at[g, t], sib)

    @pl.when(q == 0)
    def _():
        for g in range(4):
            for way in range(2):
                y_send(way, g, 0, own_w(g)).start()
            sib_send(g, y // 2, own_w(g)).start()

    def y_event(way, g, k, role):
        d = 2 * k - role
        if d > reach(way, g):
            return

        @pl.when(q == role)
        def _():
            y_recv(way, g, d).wait_recv()
            t = y_from(way, d) // 2
            if d < reach(way, g):
                y_send(way, g, d, wbuf.at[g, t, w_rows]).start()
            sib_send(g, t, wbuf.at[g, t, w_rows]).start()

    ring_cols = pl.ds(pl.multiple_of(s * HEAD, HEAD), 3 * HEAD)
    give_cols = pl.ds(pl.multiple_of(s * 3 * HEAD, HEAD), HEAD)
    take_cols = pl.ds(pl.multiple_of((1 - s) * 3 * HEAD, HEAD), HEAD)

    def z_from(way, d):
        return (z - d + NZ) % NZ if way == 0 else (z + d) % NZ

    def z_reach(way, i):
        return REACH[(way, i)]

    def z_send(way, i, d):
        ref = kvbuf.at[i, z_from(way, d), :, ring_cols]
        return remote(ref, ref, zs_s.at[way, i, d], zs_r.at[way, i, d + 1], z_dev(1 if way == 0 else -1))

    def z_recv(way, i, d):
        ref = kvbuf.at[i, z_from(way, d), :, ring_cols]
        return remote(ref, ref, zs_s.at[way, i, d], zs_r.at[way, i, d], z_dev(-1 if way == 0 else 1))

    def h_send(way, i, d):
        ref = kvbuf.at[i, z_from(way, d), :, give_cols]
        return remote(ref, ref, h_s.at[way, i, d], h_r.at[way, i, d], hx)

    def h_recv(way, i, d):
        ref = kvbuf.at[i, z_from(way, d), :, take_cols]
        return remote(ref, ref, h_s.at[way, i, d], h_r.at[way, i, d], hx)

    def z_event(way, i, d):
        z_recv(way, i, d).wait_recv()
        if d < z_reach(way, i):
            copy = z_send(way, i, d)
            copy.start()
            sends.append(copy)
        copy = h_send(way, i, d)
        copy.start()
        sends.append(copy)

    x_sends = [
        remote(x_ref.at[0, 0, :, x_cols(t, 1 - s)], xbuf.at[t, own_x_rows], x_s.at[t], x_r.at[t], sx)
        for t in range(4)
    ]
    other_x_rows = pl.ds(pl.multiple_of((1 - s) * ROWS, ROWS), ROWS)

    def start_z():
        for i, p, copy in phase:
            rows = pl.ds(pl.multiple_of(peer_x[p] * SHARD, SHARD), SHARD)
            ref = kvbuf.at[i, z, rows]
            remote(ref, ref, ph_s.at[i, p], ph_r.at[i, p], x_peers[p]).wait_recv()
        for copy in local_kv:
            copy.wait()
        for i in range(2):
            for way in range(2):
                copy = z_send(way, i, 0)
                copy.start()
                sends.append(copy)
        for copy in x_sends:
            copy.start()
            sends.append(copy)

    live_prompt = plen_ref[0]

    def update(h, score, value, first):
        best = functools.reduce(jnp.maximum, [jnp.max(v, axis=1, keepdims=True) for v in score])
        if first:
            top = jnp.broadcast_to(best, (QROWS, HEAD))
        else:
            old = top_ref[h]
            top = jnp.maximum(old, best)
            fade = jnp.exp2(old - top)
        weight = [jnp.exp2(v - top[:, :1]) for v in score]
        den = functools.reduce(
            jnp.add,
            [w[:, j * HEAD : (j + 1) * HEAD] for w in weight for j in range(w.shape[1] // HEAD)],
        )
        out = functools.reduce(
            jnp.add,
            [jnp.dot(w.astype(BF16), v, preferred_element_type=F32) for w, v in zip(weight, value)],
        )
        if not first:
            den = den + den_ref[h] * fade
            out = out + acc_ref[h] * fade
        return top, den, out

    def dot_t(a, b):
        return lax.dot_general(a, b, (((1,), (1,)), ((), ())), preferred_element_type=F32)

    def attend(blocks, first=False):
        def one(h, carry):
            cols = pl.ds(pl.multiple_of(h * HEAD, HEAD), HEAD)
            query = qs[h]
            score, value = [], []
            for zb in blocks:
                key = kvbuf[0, zb, :, cols]
                pos = zb * BLOCK + lax.broadcasted_iota(jnp.int32, (1, BLOCK), 1)
                shut = jnp.where(pos < live_prompt, 0.0, NEG)
                score.append(dot_t(query, key) * SCALE + shut)
                value.append(kvbuf[1, zb, :, cols])
            top, den, out = update(h, score, value, first)
            top_ref[h] = top
            den_ref[h] = den
            acc_ref[h] = out
            return carry

        lax.fori_loop(0, KV_HEADS, one, 0)

    def attend_distance(d):
        blocks = []
        if d < 4:
            for way in range(2):
                for i in range(2):
                    h_recv(way, i, d).wait_recv()
                blocks.append(z_from(way, d))
        else:
            h_recv(0, 0, 4).wait_recv()
            h_recv(1, 1, 4).wait_recv()
            blocks.append(z_from(0, 4))
        attend(blocks)

    order = ((y - q + NY) % NY, (y - 2 + 3 * q + NY) % NY, (y + 2 - 5 * q + NY) % NY, (y + 4 - q) % NY)

    def project(g, n):
        t = order[n] // 2
        sib_recv(g, t).wait_recv()
        if n == 0:

            @pl.when(q == 0)
            def _():
                local_w[g].wait()

        add = jnp.dot(xbuf[t], wbuf[g, t], preferred_element_type=F32)
        cols = pl.ds(g * GCOLS, GCOLS)
        if n == 0:
            pacc[:, cols] = add
        elif n < 3:
            pacc[:, cols] += add
        else:
            total = pacc[:, cols] + add
            pacc[:, cols] = total
            psend[g] = total.astype(BF16)
            copy = remote(psend.at[g], precv.at[g], p_s.at[g], p_r.at[g], sx)
            copy.start()
            sends.append(copy)

    def wait_x():
        for t in range(4):
            local_x[t].wait()
            ref = xbuf.at[t, other_x_rows]
            remote(ref, ref, x_s.at[t], x_r.at[t], sx).wait_recv()

    def join(g):
        remote(psend.at[g], precv.at[g], p_s.at[g], p_r.at[g], sx).wait_recv()
        newkv[g] = (pacc[:, g * GCOLS : (g + 1) * GCOLS] + precv[g].astype(F32)).astype(BF16)

    def attend_own():
        for copy in local_q:
            copy.wait()
        attend([z], first=True)

    def finish():
        row = lax.broadcasted_iota(jnp.int32, (QROWS, 2 * ROWS), 0) % ROWS + s * ROWS
        col = lax.broadcasted_iota(jnp.int32, (QROWS, 2 * ROWS), 1)
        shut = jnp.where(col <= row, 0.0, NEG)
        for h in range(KV_HEADS):
            cols = slice((h % 2) * HEAD, (h % 2 + 1) * HEAD)
            score = dot_t(qs[h], newkv[h // 2, :, cols]) * SCALE + shut
            _, den, out = update(h, [score], [newkv[2 + h // 2, :, cols]], False)
            out = out / jnp.sum(den, axis=1, keepdims=True)
            for g in range(GROUP):
                o_ref[:, (h * GROUP + g) * HEAD : (h * GROUP + g + 1) * HEAD] = out[
                    g * ROWS : (g + 1) * ROWS
                ].astype(BF16)

    plan = []

    def at(time, fn, *args):
        plan.append((time, len(plan), fn, args))

    at(0.0, start_z)
    at(ZS + 0.2, attend_own)
    for d in range(1, 5):
        for i in range(2):
            for way in range(2):
                if d <= z_reach(way, i):
                    at(ZS + min(2 * d - 1 + i, 7) * W, z_event, way, i, d)
        at(ZS + min(2 * d, 7) * W + 3.0, attend_distance, d)
    for role in range(2):
        for g in range(4):
            for k in (1, 2):
                for way in range(2):
                    at((g + 4 * k - 2 - role) * U, y_event, way, g, k, role)
    at(18.0, wait_x)
    for g in range(4):
        at(18.1 + g * 0.5, project, g, 0)
        at(18.2 + g * 0.5, project, g, 1)
        at((g + 6) * U + 2.0, project, g, 2)
        at((g + 6) * U + 2.1, project, g, 3)
        at((g + 6) * U + 7.0, join, g)
    for _, _, fn, args in sorted(plan, key=lambda e: e[:2]):
        fn(*args)
    finish()

    for copy in sends:
        copy.wait_send()
    for _, _, copy in phase:
        copy.wait_send()
    for role in range(2):

        @pl.when(q == role)
        def _():
            for g in range(4):
                for way in range(2):
                    if role == 0:
                        y_send(way, g, 0, own_w(g)).wait_send()
                    for k in (1, 2):
                        d = 2 * k - role
                        if d < reach(way, g):
                            y_send(way, g, d, wbuf.at[g, 0, w_rows]).wait_send()

    for g in range(4):
        for t in range(4):
            sib_send(g, t, wbuf.at[g, t, w_rows]).wait_send()


def attention(resp_x, queries, key_weight, value_weight, prompt_key, prompt_values, prompt_len):
    dma = pltpu.SemaphoreType.DMA
    any_space = pl.BlockSpec(memory_space=pl.ANY)
    return pl.pallas_call(
        kernel,
        out_shape=jax.ShapeDtypeStruct((ROWS, KV_HEADS * GROUP * HEAD), BF16),
        in_specs=[any_space] * 6 + [pl.BlockSpec(memory_space=pltpu.SMEM)],
        out_specs=pl.BlockSpec(memory_space=pltpu.VMEM),
        scratch_shapes=[
            pltpu.VMEM((2, NZ, BLOCK, KV_HEADS * HEAD), BF16),
            pltpu.VMEM((4, 4, XCOLS, GCOLS), BF16),
            pltpu.VMEM((4, 2 * ROWS, XCOLS), BF16),
            pltpu.VMEM((KV_HEADS, QROWS, HEAD), BF16),
            pltpu.VMEM((2 * ROWS, 4 * GCOLS), F32),
            pltpu.VMEM((4, 2 * ROWS, GCOLS), BF16),
            pltpu.VMEM((4, 2 * ROWS, GCOLS), BF16),
            pltpu.VMEM((4, 2 * ROWS, GCOLS), BF16),
            pltpu.VMEM((KV_HEADS, QROWS, HEAD), F32),
            pltpu.VMEM((KV_HEADS, QROWS, HEAD), F32),
            pltpu.VMEM((KV_HEADS, QROWS, HEAD), F32),
            dma((2,)), dma((KV_HEADS * GROUP,)), dma((4,)), dma((4,)),
            dma((2, 3)), dma((2, 3)),
            dma((2, 2, 5)), dma((2, 2, 5)),
            dma((2, 2, 5)), dma((2, 2, 5)),
            dma((2, 4, 5)), dma((2, 4, 5)),
            dma((4, 4)), dma((4, 4)),
            dma((4,)), dma((4,)),
            dma((4,)), dma((4,)),
        ],
        compiler_params=pltpu.CompilerParams(
            collective_id=0, has_side_effects=True, vmem_limit_bytes=56 << 20
        ),
        cost_estimate=pl.CostEstimate(flops=4_400_000_000, bytes_accessed=8_000_000, transcendentals=6_000_000),
    )(resp_x, queries, key_weight, value_weight, prompt_key, prompt_values, prompt_len)


def local(
    resp_x, queries, key_weight, value_weight, prompt_key, cached_prompt_values, lengths, prompt_len
):
    mixed = attention(
        resp_x, queries, key_weight, value_weight, prompt_key, cached_prompt_values, prompt_len
    )
    row = lax.axis_index("seq") * ROWS + jnp.arange(ROWS, dtype=jnp.int32)
    live = (row < lengths[0, 0])[:, None]
    return jnp.where(live, mixed, jnp.zeros((), BF16))[None, None]


def solution(mesh):
    return jax.shard_map(
        local,
        mesh=mesh,
        in_specs=(
            P("blk", "pair", "seq", None),
            P("blk", "pair", "seq", None),
            P("blk", None),
            P("blk", None),
            P("blk", ("pair", "seq"), None),
            P("blk", ("pair", "seq"), None),
            P("blk", "pair"),
            P("blk"),
        ),
        out_specs=P("blk", "pair", "seq", None),
        check_vma=False,
    )
```

```python
import functools
import math

import jax
import jax.numpy as jnp
from jax import lax
from jax.experimental import pallas as pl
from jax.experimental.pallas import tpu as pltpu
from jax.sharding import PartitionSpec as P

KV_HEADS = 4
HEAD = 128
GROUP = 5
NY, NZ, NX = 8, 8, 4
ROWS = 128
SHARD = 64
BLOCK = NX * SHARD
WROWS = 320
XCOLS = 2 * WROWS
WCOLS = HEAD
QROWS = GROUP * ROWS
NEG = -1e30
SCALE = HEAD ** (-0.5) * math.log2(math.e)
MESH = pl.DeviceIdType.MESH
F32 = jnp.float32
BF16 = jnp.bfloat16
LIMIT = dict(z=6, y=5, hx=4, sx=3, sib=8)
HOP = 5.5
WAVES = (0.0, 0.3, 0.6, 0.9)
XTIME = (0.0, 3.5, 4.5, 7.0)
ZTIME = (6.5, 10.5, 11.5, 14.0)
ZHOP = (5.0, 6.5, 6.5, 6.5)
REACH = ((4, 3), (3, 4))
WAVE_HEADS = (1, 2, 0, 3)


def kernel(
    x_ref, q_ref, kw_ref, vw_ref, pk_ref, pv_ref, plen_ref, o_ref,
    kvbuf, wbuf, xin, xsend, xbuf, qs, pacc, psend, precv, newkv, top_ref, den_ref, acc_ref,
    own_sem, q_sem, xl_sem, wl_sem,
    ph_s, ph_r, zs_s, zs_r, zt_s, zt_r, h_s, h_r, y_s, y_r, b_s, b_r, x_s, x_r, p_s, p_r,
):
    blk, pair, s = lax.axis_index("blk"), lax.axis_index("pair"), lax.axis_index("seq")
    y, c = blk // 2, blk % 2
    z, hi = pair // 2, pair % 2
    x = hi * 2 + s
    up = 1 - 2 * (y % 2)
    heads = (1, 2, 3 * s, 3 * (1 - s))
    lanes = tuple(pl.ds(pl.multiple_of(h * HEAD, HEAD), HEAD) for h in heads)

    def y_dev(step):
        return {"blk": ((y + step + NY) % NY) * 2 + c, "pair": pair, "seq": s}

    def z_dev(step):
        return {"blk": blk, "pair": ((z + step + NZ) % NZ) * 2 + hi, "seq": s}

    sib = {"blk": y * 2 + (1 - c), "pair": pair, "seq": s}
    sx = {"blk": blk, "pair": pair, "seq": 1 - s}
    hx = {"blk": blk, "pair": z * 2 + (1 - hi), "seq": 1 - s}
    x2 = {"blk": blk, "pair": z * 2 + (1 - hi), "seq": s}
    x_peers = (sx, hx, x2)

    def slot(p):
        return pl.ds((p + 1) * SHARD, SHARD)

    def remote(src, dst, ss, rs, dev):
        return pltpu.make_async_remote_copy(
            src_ref=src, dst_ref=dst, send_sem=ss, recv_sem=rs, device_id=dev, device_id_type=MESH
        )

    flying = {}

    def go(link, copy, start=True):
        queue = flying.setdefault(link, [])
        if len(queue) >= LIMIT[link[0]]:
            queue.pop(0).wait_send()
        if start:
            copy.start()
        queue.append(copy)


    local_q = [
        pltpu.make_async_copy(
            q_ref.at[0, 0, :, pl.ds(pl.multiple_of((heads[n] * GROUP + g) * HEAD, HEAD), HEAD)],
            qs.at[n, pl.ds(g * ROWS, ROWS)],
            q_sem.at[n * GROUP + g],
        )
        for n in range(KV_HEADS)
        for g in range(GROUP)
    ]
    cached = (pk_ref, pv_ref)
    own_rows = pl.ds(0, SHARD)
    local_kv = [
        pltpu.make_async_copy(cached[i].at[0], kvbuf.at[i, z, own_rows], own_sem.at[i]) for i in range(2)
    ]
    own_x_rows = pl.ds(pl.multiple_of(s * ROWS, ROWS), ROWS)
    local_x = pltpu.make_async_copy(x_ref.at[0, 0], xin, xl_sem.at[0])
    weights = (kw_ref, vw_ref)

    def w_cols(g):
        return weights[g // KV_HEADS].at[:, pl.ds((g % KV_HEADS) * WCOLS, WCOLS)]

    def w_ref(g, yy):
        kv, n = g if isinstance(g, tuple) else divmod(g, KV_HEADS)
        rows = pl.ds(pl.multiple_of((yy % 2) * WROWS, 64), WROWS)
        return wbuf.at[kv, yy // 2, rows, pl.ds(n * WCOLS, WCOLS)]

    owner = c * 2 + s

    def local_w(g):
        return pltpu.make_async_copy(w_cols(g), w_ref(g, y), wl_sem.at[g])

    local_x.start()
    for copy in local_kv + local_q:
        copy.start()

    @pl.when(c == s)
    def _():
        for g in range(2 * KV_HEADS):
            local_w(g).start()

    barrier = pltpu.get_barrier_semaphore()
    for dev in (sib, sx, hx, x2, y_dev(1), y_dev(-1), z_dev(1), z_dev(-1)):
        pl.semaphore_signal(barrier, inc=1, device_id=dev, device_id_type=MESH)
    pl.semaphore_wait(barrier, 8)

    phase = []
    for p in (0, 1, 2):
        for i in range(2):
            copy = remote(cached[i].at[0], kvbuf.at[i, z, slot(p)], ph_s.at[i, p], ph_r.at[i, p], x_peers[p])
            copy.start()
            phase.append((i, p, copy))

    def y_from(way, d):
        return (y - d + NY) % NY if way == 0 else (y + d) % NY

    def y_send(way, n, d, src=None):
        ref = w_ref((c, n), y_from(way, d))
        return remote(
            ref if src is None else src, ref, y_s.at[way, n, d], y_r.at[way, n, d + 1], y_dev(1 - 2 * way)
        )

    def y_recv(way, n, d):
        ref = w_ref((c, n), y_from(way, d))
        return remote(ref, ref, y_s.at[way, n, d], y_r.at[way, n, d], y_dev(2 * way - 1))

    def sib_copy(g, yy, src=None):
        ref = w_ref(g, yy)
        kv, n = g if isinstance(g, tuple) else divmod(g, KV_HEADS)
        return remote(ref if src is None else src, ref, b_s.at[kv, n, yy], b_r.at[kv, n, yy], sib)

    def y_start(n):
        for way in range(2):
            go(("y", way), y_send(way, n, 0), start=False)
        for cc in range(2):

            @pl.when(owner == 3 * cc)
            def _():
                for way in range(2):
                    y_send(way, n, 0, w_cols(KV_HEADS * cc + n)).start()

            @pl.when(owner == 2 - cc)
            def _():
                sib_copy((c, n), y).wait_recv()
                for way in range(2):
                    y_send(way, n, 0).start()

    for cc in range(2):

        @pl.when(owner == 3 * cc)
        def _():
            for kv in (1 - cc, cc):
                for n in WAVE_HEADS:
                    sib_copy(KV_HEADS * kv + n, y, w_cols(KV_HEADS * kv + n)).start()

    def y_event(way, n, d):
        y_recv(way, n, d).wait_recv()
        if d < REACH[way][n % 2]:
            go(("y", way), y_send(way, n, d))
        go(("sib",), sib_copy((c, n), y_from(way, d)))

    ring_cols = pl.ds(pl.multiple_of(s * HEAD, HEAD), 3 * HEAD)
    give_cols = pl.ds(pl.multiple_of(s * 3 * HEAD, HEAD), HEAD)
    take_cols = pl.ds(pl.multiple_of((1 - s) * 3 * HEAD, HEAD), HEAD)

    def z_from(way, d):
        return (z - d + NZ) % NZ if way == 0 else (z + d) % NZ

    def z_reach(way, i):
        return REACH[way][i]

    def z_ref(stream, way, i, d):
        return kvbuf.at[i, z_from(way, d), pl.ds(stream * SHARD, SHARD), ring_cols]

    def z_send(stream, way, i, d, src=None):
        ref = z_ref(stream, way, i, d)
        return remote(
            ref if src is None else src, ref, zs_s.at[stream, way, i, d], zs_r.at[stream, way, i, d + 1],
            z_dev(1 - 2 * way),
        )

    def z_recv(stream, way, i, d):
        ref = z_ref(stream, way, i, d)
        return remote(ref, ref, zs_s.at[stream, way, i, d], zs_r.at[stream, way, i, d], z_dev(2 * way - 1))

    def h_send(way, i, d):
        ref = kvbuf.at[i, z_from(way, d), :, give_cols]
        return remote(ref, ref, h_s.at[way, i, d], h_r.at[way, i, d], hx)

    def h_recv(way, i, d):
        ref = kvbuf.at[i, z_from(way, d), :, take_cols]
        return remote(ref, ref, h_s.at[way, i, d], h_r.at[way, i, d], hx)

    def z_event(stream, way, i, d):
        z_recv(stream, way, i, d).wait_recv()
        if d < z_reach(way, i):
            go(("z", way), z_send(stream, way, i, d))
        if stream == NX - 1 and d < 4:
            go(("hx",), h_send(way, i, d))

    def take_send(i, d):
        ref = kvbuf.at[i, z_from(i, d), :, take_cols]
        return remote(ref, ref, zt_s.at[i], zt_r.at[i], z_dev(1 - 2 * i))

    def take_event(i):
        h_recv(i, i, 3).wait_recv()
        go(("z", i), take_send(i, 3))

    order = (y, (y - up + NY) % NY, (y + 2 * up + NY) % NY, (y + 4) % NY)

    def x_part(t, parity):
        first = 2 * t * XCOLS + parity * WROWS
        return jnp.concatenate(
            [xin[:, first : first + WROWS], xin[:, first + XCOLS : first + XCOLS + WROWS]], axis=1
        )

    def split_x():
        local_x.wait()
        for parity in range(2):

            @pl.when(s == parity)
            def _():
                for t in range(4):
                    xsend[t] = x_part(t, 1 - parity)
                    xbuf[t, parity * ROWS : (parity + 1) * ROWS] = x_part(t, parity)

    def send_x(first, last):
        for yy in order[first:last]:
            t = yy // 2
            go(("sx",), remote(xsend.at[t], xbuf.at[t, own_x_rows], x_s.at[t], x_r.at[t], sx))

    other_x_rows = pl.ds(pl.multiple_of((1 - s) * ROWS, ROWS), ROWS)

    def z_start(stream, i):
        if stream > 0:
            ref = kvbuf.at[i, z, slot(stream - 1)]
            remote(ref, ref, ph_s.at[i, stream - 1], ph_r.at[i, stream - 1], x_peers[stream - 1]).wait_recv()
        for way in range(2):
            go(("z", way), z_send(stream, way, i, 0, cached[i].at[0, :, ring_cols] if stream == 0 else None))

    live_prompt = plen_ref[0]

    def update(h, score, value, first):
        best = functools.reduce(jnp.maximum, [jnp.max(v, axis=1, keepdims=True) for v in score])
        if first:
            top = jnp.broadcast_to(best, (QROWS, HEAD))
        else:
            old = top_ref[h]
            top = jnp.maximum(old, best)
            fade = jnp.exp2(old - top)
        weight = [jnp.exp2(v - top[:, :1]) for v in score]
        den = functools.reduce(
            jnp.add,
            [w[:, j * HEAD : (j + 1) * HEAD] for w in weight for j in range(w.shape[1] // HEAD)],
        )
        out = functools.reduce(
            jnp.add,
            [jnp.dot(w.astype(BF16), v, preferred_element_type=F32) for w, v in zip(weight, value)],
        )
        if not first:
            den = den + den_ref[h] * fade
            out = out + acc_ref[h] * fade
        return top, den, out

    def dot_t(a, b):
        return lax.dot_general(a, b, (((1,), (1,)), ((), ())), preferred_element_type=F32)

    def prompt_piece(n, d, zb):
        away = int(d > 0 and n == KV_HEADS - 1)
        ehi, es = (1 - hi, 1 - s) if away else (hi, s)
        col = lax.broadcasted_iota(jnp.int32, (1, BLOCK), 1)
        shard = jnp.where(
            col < SHARD,
            ehi * 2 + es,
            jnp.where(
                col < 2 * SHARD,
                ehi * 2 + 1 - es,
                jnp.where(col < 3 * SHARD, (1 - ehi) * 2 + 1 - es, (1 - ehi) * 2 + es),
            ),
        )
        pos = zb * BLOCK + shard * SHARD + col % SHARD
        shut = jnp.where(pos < live_prompt, 0.0, NEG)
        return dot_t(qs[n], kvbuf[0, zb, :, lanes[n]]) * SCALE + shut, kvbuf[1, zb, :, lanes[n]]

    def attend(h, d):
        blocks = [z] if d == 0 else [z_from(way, d) for way in range(2)]
        score, value = zip(*(prompt_piece(h, d, zb) for zb in blocks))
        top, den, out = update(h, score, value, d == 0)
        top_ref[h] = top
        den_ref[h] = den
        acc_ref[h] = out

    def wait_own():
        for copy in local_q + local_kv:
            copy.wait()

    def wait_neighbour(d):
        for way in range(2):
            for i in range(2):
                if d == 4 and way == 0:
                    take_send(i, 4).wait_recv()
                if d < 3 or (d == 3 and way != i):
                    h_recv(way, i, d).wait_recv()

    def project(m, p):
        kv = c if m == 0 else 1 - c
        t = order[p] // 2
        if p == 0:

            @pl.when(c == s)
            def _():
                for n in range(KV_HEADS):
                    pltpu.make_async_copy(w_cols(n), w_ref((kv, n), y), wl_sem.at[kv * KV_HEADS + n]).wait()

            if m == 1:

                @pl.when(c != s)
                def _():
                    for n in range(KV_HEADS):
                        sib_copy((kv, n), y).wait_recv()

        if m == 1:
            for n in range(KV_HEADS):
                if p > 0:
                    sib_copy((kv, n), order[p]).wait_recv()
                sib_copy((kv, n), 4 * t + 1 - order[p]).wait_recv()
        if m == 0:
            ref = xbuf.at[t, other_x_rows]
            remote(ref, ref, x_s.at[t], x_r.at[t], sx).wait_recv()
        if p < 3:
            add = jnp.dot(xbuf[t], wbuf[kv, t], preferred_element_type=F32)
            pacc[kv] = add if p == 0 else pacc[kv] + add
        else:
            for half in range(2):
                cols = slice(half * 2 * HEAD, (half + 1) * 2 * HEAD)
                total = pacc[kv, :, cols] + jnp.dot(xbuf[t], wbuf[kv, t, :, cols], preferred_element_type=F32)
                pacc[kv, :, cols] = total
                psend[kv, half] = total.astype(BF16)
                go(("sx",), part_copy(kv, half))

    def part_copy(kv, half):
        return remote(psend.at[kv, half], precv.at[kv, half], p_s.at[kv, half], p_r.at[kv, half], sx)

    def join(half):
        cols = slice(half * 2 * HEAD, (half + 1) * 2 * HEAD)
        for kv in range(2):
            part_copy(kv, half).wait_recv()
            newkv[kv, :, cols] = (pacc[kv, :, cols] + precv[kv, half].astype(F32)).astype(BF16)

    def finish(n):
        row = lax.broadcasted_iota(jnp.int32, (QROWS, 2 * ROWS), 0) % ROWS + s * ROWS
        col = lax.broadcasted_iota(jnp.int32, (QROWS, 2 * ROWS), 1)
        shut = jnp.where(col <= row, 0.0, NEG)
        score, value = prompt_piece(n, 4, z_from(0, 4))
        new_score = dot_t(qs[n], newkv[0, :, lanes[n]]) * SCALE + shut
        _, den, out = update(n, [score, new_score], [value, newkv[1, :, lanes[n]]], False)
        out = out / jnp.sum(den, axis=1, keepdims=True)
        for g in range(GROUP):
            cols = pl.ds(pl.multiple_of((heads[n] * GROUP + g) * HEAD, HEAD), HEAD)
            o_ref[:, cols] = out[g * ROWS : (g + 1) * ROWS].astype(BF16)

    events, tasks = [], []

    def event(time, fn, *args):
        events.append((time, len(events), fn, args))

    def task(time, length, fn, *args):
        tasks.append((time, length, fn, args))

    for stream in range(NX):
        for i in range(2):
            event(XTIME[stream] + 0.5 * i, z_start, stream, i)
            for way in range(2):
                for d in range(1, z_reach(way, i) + 1):
                    event(ZTIME[stream] + ZHOP[stream] * (d - 1) + 0.5 * i, z_event, stream, way, i, d)
    event(0.6, split_x)
    event(XTIME[2] + 0.6, send_x, 0, 1)
    event(XTIME[3] + 0.6, send_x, 1, 4)
    full = [ZTIME[3] + ZHOP[3] * (d - 1) + 0.6 for d in range(5)]
    event(full[3] + 3.5, take_event, 0)
    event(full[3] + 4.0, take_event, 1)
    for wave, n in zip(WAVES, WAVE_HEADS):
        event(wave + 2.0, y_start, n)
        for way in range(2):
            for d in range(1, REACH[way][n % 2] + 1):
                event(wave + 2.5 + HOP * d, y_event, way, n, d)
    for p in range(4):
        for m in range(2):
            ready = max(11.0 + 3.5 * p, WAVES[3] + 2.6 + HOP * (p + 1) + 2.5 * m)
            task(ready, 0.7, project, m, p)
    for half in range(2):
        task(ready + 6.0 + 2.0 * half, 0.5, join, half)
    task(9.0, 0.0, wait_own)
    for d in range(4):
        ready = 9.0 if d == 0 else full[d]
        for n in range(KV_HEADS):
            if d and n == KV_HEADS - 1:
                ready += 4.1
                task(ready, 0.0, wait_neighbour, d)
            task(ready, 0.7 if d else 0.4, attend, n, d)
    tasks.sort(key=lambda e: (e[2] not in (project, join), e[0]))
    events.sort(key=lambda e: e[:2])
    now = 0.0
    while events or tasks:
        ready = [t for t in tasks if t[0] <= now]
        if events and events[0][0] <= now:
            _, _, fn, args = events.pop(0)
            fn(*args)
            now += 0.1
        elif ready:
            tasks.remove(ready[0])
            _, length, fn, args = ready[0]
            fn(*args)
            now += length
        else:
            now = min([e[0] for e in events[:1]] + [t[0] for t in tasks])
    for n in range(KV_HEADS):
        if n == KV_HEADS - 1:
            wait_neighbour(4)
        finish(n)

    for queue in flying.values():
        for copy in queue:
            copy.wait_send()
    for _, _, copy in phase:
        copy.wait_send()

    @pl.when(c == s)
    def _():
        for g in range(2 * KV_HEADS):
            sib_copy(g, y).wait_send()


def attention(resp_x, queries, key_weight, value_weight, prompt_key, prompt_values, prompt_len):
    dma = pltpu.SemaphoreType.DMA
    any_space = pl.BlockSpec(memory_space=pl.ANY)
    return pl.pallas_call(
        kernel,
        out_shape=jax.ShapeDtypeStruct((ROWS, KV_HEADS * GROUP * HEAD), BF16),
        in_specs=[any_space] * 6 + [pl.BlockSpec(memory_space=pltpu.SMEM)],
        out_specs=pl.BlockSpec(memory_space=pltpu.VMEM),
        scratch_shapes=[
            pltpu.VMEM((2, NZ, BLOCK, KV_HEADS * HEAD), BF16),
            pltpu.VMEM((2, 4, XCOLS, 4 * WCOLS), BF16),
            pltpu.VMEM((ROWS, 8 * XCOLS), BF16),
            pltpu.VMEM((4, ROWS, XCOLS), BF16),
            pltpu.VMEM((4, 2 * ROWS, XCOLS), BF16),
            pltpu.VMEM((KV_HEADS, QROWS, HEAD), BF16),
            pltpu.VMEM((2, 2 * ROWS, 4 * WCOLS), F32),
            pltpu.VMEM((2, 2, 2 * ROWS, 2 * WCOLS), BF16),
            pltpu.VMEM((2, 2, 2 * ROWS, 2 * WCOLS), BF16),
            pltpu.VMEM((2, 2 * ROWS, 4 * WCOLS), BF16),
            pltpu.VMEM((KV_HEADS, QROWS, HEAD), F32),
            pltpu.VMEM((KV_HEADS, QROWS, HEAD), F32),
            pltpu.VMEM((KV_HEADS, QROWS, HEAD), F32),
            dma((2,)), dma((KV_HEADS * GROUP,)), dma((1,)), dma((8,)),
            dma((2, 3)), dma((2, 3)),
            dma((4, 2, 2, 5)), dma((4, 2, 2, 5)),
            dma((2,)), dma((2,)),
            dma((2, 2, 5)), dma((2, 2, 5)),
            dma((2, 4, 5)), dma((2, 4, 5)),
            dma((2, 4, 8)), dma((2, 4, 8)),
            dma((4,)), dma((4,)),
            dma((2, 2)), dma((2, 2)),
        ],
        compiler_params=pltpu.CompilerParams(
            collective_id=0, has_side_effects=True, vmem_limit_bytes=56 << 20
        ),
        cost_estimate=pl.CostEstimate(flops=4_400_000_000, bytes_accessed=8_000_000, transcendentals=6_000_000),
    )(resp_x, queries, key_weight, value_weight, prompt_key, prompt_values, prompt_len)


def local(
    resp_x, queries, key_weight, value_weight, prompt_key, cached_prompt_values, lengths, prompt_len
):
    mixed = attention(
        resp_x, queries, key_weight, value_weight, prompt_key, cached_prompt_values, prompt_len
    )
    row = lax.axis_index("seq") * ROWS + jnp.arange(ROWS, dtype=jnp.int32)
    live = (row < lengths[0, 0])[:, None]
    return jnp.where(live, mixed, jnp.zeros((), BF16))[None, None]


def solution(mesh):
    return jax.shard_map(
        local,
        mesh=mesh,
        in_specs=(
            P("blk", "pair", "seq", None),
            P("blk", "pair", "seq", None),
            P("blk", None),
            P("blk", None),
            P("blk", ("pair", "seq"), None),
            P("blk", ("pair", "seq"), None),
            P("blk", "pair"),
            P("blk"),
        ),
        out_specs=P("blk", "pair", "seq", None),
        check_vma=False,
    )
```

```python
import functools
import math

import jax
import jax.numpy as jnp
from jax import lax
from jax.experimental import pallas as pl
from jax.experimental.pallas import tpu as pltpu
from jax.sharding import PartitionSpec as P

KV_HEADS = 4
HEAD = 128
GROUP = 5
NY, NZ, NX = 8, 8, 4
ROWS = 128
SHARD = 64
BLOCK = NX * SHARD
WROWS = 320
XCOLS = 2 * WROWS
WCOLS = HEAD
QROWS = GROUP * ROWS
NEG = -1e30
SCALE = HEAD ** (-0.5) * math.log2(math.e)
MESH = pl.DeviceIdType.MESH
F32 = jnp.float32
BF16 = jnp.bfloat16
LIMIT = dict(z=6, y=5, hx=4, sx=3, sib=8)
HOP = 5.5
WAVES = (0.0, 0.3, 0.6, 0.9)
XTIME = (0.0, 3.5, 4.5, 7.0)
ZTIME = (6.5, 10.5, 11.5, 14.0)
ZHOP = (5.0, 6.5, 6.5, 6.5)
REACH = ((4, 3), (3, 4))
WAVE_HEADS = (1, 2, 0, 3)


def kernel(
    x_ref, q_ref, kw_ref, vw_ref, pk_ref, pv_ref, plen_ref, o_ref,
    kvbuf, wbuf, xin, xsend, xbuf, qs, pacc, psend, precv, newkv, top_ref, den_ref, acc_ref,
    own_sem, q_sem, xl_sem, wl_sem,
    ph_s, ph_r, zs_s, zs_r, zt_s, zt_r, h_s, h_r, y_s, y_r, b_s, b_r, x_s, x_r, p_s, p_r,
):
    blk, pair, s = lax.axis_index("blk"), lax.axis_index("pair"), lax.axis_index("seq")
    y, c = blk // 2, blk % 2
    z, hi = pair // 2, pair % 2
    x = hi * 2 + s
    up = 1 - 2 * (y % 2)
    heads = (1, 2, 3 * s, 3 * (1 - s))
    lanes = tuple(pl.ds(pl.multiple_of(h * HEAD, HEAD), HEAD) for h in heads)

    def y_dev(step):
        return {"blk": ((y + step + NY) % NY) * 2 + c, "pair": pair, "seq": s}

    def z_dev(step):
        return {"blk": blk, "pair": ((z + step + NZ) % NZ) * 2 + hi, "seq": s}

    sib = {"blk": y * 2 + (1 - c), "pair": pair, "seq": s}
    sx = {"blk": blk, "pair": pair, "seq": 1 - s}
    hx = {"blk": blk, "pair": z * 2 + (1 - hi), "seq": 1 - s}
    x2 = {"blk": blk, "pair": z * 2 + (1 - hi), "seq": s}
    x_peers = (sx, hx, x2)

    def slot(p):
        return pl.ds((p + 1) * SHARD, SHARD)

    def remote(src, dst, ss, rs, dev):
        return pltpu.make_async_remote_copy(
            src_ref=src, dst_ref=dst, send_sem=ss, recv_sem=rs, device_id=dev, device_id_type=MESH
        )

    flying = {}

    def go(link, copy, start=True):
        queue = flying.setdefault(link, [])
        if len(queue) >= LIMIT[link[0]]:
            queue.pop(0).wait_send()
        if start:
            copy.start()
        queue.append(copy)


    local_q = [
        pltpu.make_async_copy(
            q_ref.at[0, 0, :, pl.ds(pl.multiple_of((heads[n] * GROUP + g) * HEAD, HEAD), HEAD)],
            qs.at[n, pl.ds(g * ROWS, ROWS)],
            q_sem.at[n * GROUP + g],
        )
        for n in range(KV_HEADS)
        for g in range(GROUP)
    ]
    cached = (pk_ref, pv_ref)
    own_rows = pl.ds(0, SHARD)
    local_kv = [
        pltpu.make_async_copy(cached[i].at[0], kvbuf.at[i, z, own_rows], own_sem.at[i]) for i in range(2)
    ]
    own_x_rows = pl.ds(pl.multiple_of(s * ROWS, ROWS), ROWS)
    local_x = pltpu.make_async_copy(x_ref.at[0, 0], xin, xl_sem.at[0])
    weights = (kw_ref, vw_ref)

    def w_cols(g):
        return weights[g // KV_HEADS].at[:, pl.ds((g % KV_HEADS) * WCOLS, WCOLS)]

    def w_ref(g, yy):
        kv, n = g if isinstance(g, tuple) else divmod(g, KV_HEADS)
        rows = pl.ds(pl.multiple_of((yy % 2) * WROWS, 64), WROWS)
        return wbuf.at[kv, yy // 2, rows, pl.ds(n * WCOLS, WCOLS)]

    owner = c * 2 + s

    def local_w(g):
        return pltpu.make_async_copy(w_cols(g), w_ref(g, y), wl_sem.at[g])

    local_x.start()
    for copy in local_kv + local_q:
        copy.start()

    @pl.when(c == s)
    def _():
        for g in range(2 * KV_HEADS):
            local_w(g).start()

    barrier = pltpu.get_barrier_semaphore()
    for dev in (sib, sx, hx, x2, y_dev(1), y_dev(-1), z_dev(1), z_dev(-1)):
        pl.semaphore_signal(barrier, inc=1, device_id=dev, device_id_type=MESH)
    pl.semaphore_wait(barrier, 8)

    phase = []
    for p in (0, 1, 2):
        for i in range(2):
            copy = remote(cached[i].at[0], kvbuf.at[i, z, slot(p)], ph_s.at[i, p], ph_r.at[i, p], x_peers[p])
            copy.start()
            phase.append((i, p, copy))

    def y_from(way, d):
        return (y - d + NY) % NY if way == 0 else (y + d) % NY

    def y_send(way, n, d, src=None):
        ref = w_ref((c, n), y_from(way, d))
        return remote(
            ref if src is None else src, ref, y_s.at[way, n, d], y_r.at[way, n, d + 1], y_dev(1 - 2 * way)
        )

    def y_recv(way, n, d):
        ref = w_ref((c, n), y_from(way, d))
        return remote(ref, ref, y_s.at[way, n, d], y_r.at[way, n, d], y_dev(2 * way - 1))

    def sib_copy(g, yy, src=None):
        ref = w_ref(g, yy)
        kv, n = g if isinstance(g, tuple) else divmod(g, KV_HEADS)
        return remote(ref if src is None else src, ref, b_s.at[kv, n, yy], b_r.at[kv, n, yy], sib)

    def y_start(n):
        for way in range(2):
            go(("y", way), y_send(way, n, 0), start=False)
        for cc in range(2):

            @pl.when(owner == 3 * cc)
            def _():
                for way in range(2):
                    y_send(way, n, 0, w_cols(KV_HEADS * cc + n)).start()

            @pl.when(owner == 2 - cc)
            def _():
                sib_copy((c, n), y).wait_recv()
                for way in range(2):
                    y_send(way, n, 0).start()

    for cc in range(2):

        @pl.when(owner == 3 * cc)
        def _():
            for kv in (1 - cc, cc):
                for n in WAVE_HEADS:
                    sib_copy(KV_HEADS * kv + n, y, w_cols(KV_HEADS * kv + n)).start()

    def y_event(way, n, d):
        y_recv(way, n, d).wait_recv()
        if d < REACH[way][n % 2]:
            go(("y", way), y_send(way, n, d))
        go(("sib",), sib_copy((c, n), y_from(way, d)))

    ring_cols = pl.ds(pl.multiple_of(s * HEAD, HEAD), 3 * HEAD)
    give_cols = pl.ds(pl.multiple_of(s * 3 * HEAD, HEAD), HEAD)
    take_cols = pl.ds(pl.multiple_of((1 - s) * 3 * HEAD, HEAD), HEAD)

    def z_from(way, d):
        return (z - d + NZ) % NZ if way == 0 else (z + d) % NZ

    def z_reach(way, i):
        return REACH[way][i]

    def z_ref(stream, way, i, d):
        return kvbuf.at[i, z_from(way, d), pl.ds(stream * SHARD, SHARD), ring_cols]

    def z_send(stream, way, i, d, src=None):
        ref = z_ref(stream, way, i, d)
        return remote(
            ref if src is None else src, ref, zs_s.at[stream, way, i, d], zs_r.at[stream, way, i, d + 1],
            z_dev(1 - 2 * way),
        )

    def z_recv(stream, way, i, d):
        ref = z_ref(stream, way, i, d)
        return remote(ref, ref, zs_s.at[stream, way, i, d], zs_r.at[stream, way, i, d], z_dev(2 * way - 1))

    def h_send(way, i, d):
        ref = kvbuf.at[i, z_from(way, d), :, give_cols]
        return remote(ref, ref, h_s.at[way, i, d], h_r.at[way, i, d], hx)

    def h_recv(way, i, d):
        ref = kvbuf.at[i, z_from(way, d), :, take_cols]
        return remote(ref, ref, h_s.at[way, i, d], h_r.at[way, i, d], hx)

    def z_event(stream, way, i, d):
        z_recv(stream, way, i, d).wait_recv()
        if d < z_reach(way, i):
            go(("z", way), z_send(stream, way, i, d))
        if stream == NX - 1 and d < 4:
            go(("hx",), h_send(way, i, d))

    def take_send(i, d):
        ref = kvbuf.at[i, z_from(i, d), :, take_cols]
        return remote(ref, ref, zt_s.at[i], zt_r.at[i], z_dev(1 - 2 * i))

    def take_event(i):
        h_recv(i, i, 3).wait_recv()
        go(("z", i), take_send(i, 3))

    order = (y, (y - up + NY) % NY, (y + 2 * up + NY) % NY, (y + 4) % NY)

    def x_part(t, parity):
        first = 2 * t * XCOLS + parity * WROWS
        return jnp.concatenate(
            [xin[:, first : first + WROWS], xin[:, first + XCOLS : first + XCOLS + WROWS]], axis=1
        )

    def split_x():
        local_x.wait()
        for parity in range(2):

            @pl.when(s == parity)
            def _():
                for t in range(4):
                    xsend[t] = x_part(t, 1 - parity)
                    xbuf[t, parity * ROWS : (parity + 1) * ROWS] = x_part(t, parity)

    def send_x(first, last):
        for yy in order[first:last]:
            t = yy // 2
            go(("sx",), remote(xsend.at[t], xbuf.at[t, own_x_rows], x_s.at[t], x_r.at[t], sx))

    other_x_rows = pl.ds(pl.multiple_of((1 - s) * ROWS, ROWS), ROWS)

    def z_start(stream, i):
        if stream > 0:
            ref = kvbuf.at[i, z, slot(stream - 1)]
            remote(ref, ref, ph_s.at[i, stream - 1], ph_r.at[i, stream - 1], x_peers[stream - 1]).wait_recv()
        for way in range(2):
            go(("z", way), z_send(stream, way, i, 0, cached[i].at[0, :, ring_cols] if stream == 0 else None))

    live_prompt = plen_ref[0]

    def update(h, score, value, first):
        best = functools.reduce(jnp.maximum, [jnp.max(v, axis=1, keepdims=True) for v in score])
        if first:
            top = jnp.broadcast_to(best, (QROWS, HEAD))
        else:
            old = top_ref[h]
            top = jnp.maximum(old, best)
            fade = jnp.exp2(old - top)
        weight = [jnp.exp2(v - top[:, :1]) for v in score]
        den = functools.reduce(
            jnp.add,
            [w[:, j * HEAD : (j + 1) * HEAD] for w in weight for j in range(w.shape[1] // HEAD)],
        )
        out = functools.reduce(
            jnp.add,
            [jnp.dot(w.astype(BF16), v, preferred_element_type=F32) for w, v in zip(weight, value)],
        )
        if not first:
            den = den + den_ref[h] * fade
            out = out + acc_ref[h] * fade
        return top, den, out

    def dot_t(a, b):
        return lax.dot_general(a, b, (((1,), (1,)), ((), ())), preferred_element_type=F32)

    def prompt_piece(n, d, zb):
        away = int(d > 0 and n == KV_HEADS - 1)
        ehi, es = (1 - hi, 1 - s) if away else (hi, s)
        col = lax.broadcasted_iota(jnp.int32, (1, BLOCK), 1)
        shard = jnp.where(
            col < SHARD,
            ehi * 2 + es,
            jnp.where(
                col < 2 * SHARD,
                ehi * 2 + 1 - es,
                jnp.where(col < 3 * SHARD, (1 - ehi) * 2 + 1 - es, (1 - ehi) * 2 + es),
            ),
        )
        pos = zb * BLOCK + shard * SHARD + col % SHARD
        shut = jnp.where(pos < live_prompt, 0.0, NEG)
        return dot_t(qs[n], kvbuf[0, zb, :, lanes[n]]) * SCALE + shut, kvbuf[1, zb, :, lanes[n]]

    def attend(h, d):
        blocks = [z] if d == 0 else [z_from(way, d) for way in range(2)]
        score, value = zip(*(prompt_piece(h, d, zb) for zb in blocks))
        top, den, out = update(h, score, value, d == 0)
        top_ref[h] = top
        den_ref[h] = den
        acc_ref[h] = out

    def wait_own():
        for copy in local_q + local_kv:
            copy.wait()

    def wait_neighbour(d):
        for way in range(2):
            for i in range(2):
                if d == 4 and way == 0:
                    take_send(i, 4).wait_recv()
                if d < 3 or (d == 3 and way != i):
                    h_recv(way, i, d).wait_recv()

    def project(m, p):
        kv = c if m == 0 else 1 - c
        t = order[p] // 2
        if p == 0:

            @pl.when(c == s)
            def _():
                for n in range(KV_HEADS):
                    pltpu.make_async_copy(w_cols(n), w_ref((kv, n), y), wl_sem.at[kv * KV_HEADS + n]).wait()

            if m == 1:

                @pl.when(c != s)
                def _():
                    for n in range(KV_HEADS):
                        sib_copy((kv, n), y).wait_recv()

        if m == 1:
            for n in range(KV_HEADS):
                if p > 0:
                    sib_copy((kv, n), order[p]).wait_recv()
                sib_copy((kv, n), 4 * t + 1 - order[p]).wait_recv()
        if m == 0:
            ref = xbuf.at[t, other_x_rows]
            remote(ref, ref, x_s.at[t], x_r.at[t], sx).wait_recv()
        if p < 3:
            add = jnp.dot(xbuf[t], wbuf[kv, t], preferred_element_type=F32)
            pacc[kv] = add if p == 0 else pacc[kv] + add
        else:
            for half in range(2):
                cols = slice(half * 2 * HEAD, (half + 1) * 2 * HEAD)
                total = pacc[kv, :, cols] + jnp.dot(xbuf[t], wbuf[kv, t, :, cols], preferred_element_type=F32)
                pacc[kv, :, cols] = total
                psend[kv, half] = total.astype(BF16)
                go(("sx",), part_copy(kv, half))

    def part_copy(kv, half):
        return remote(psend.at[kv, half], precv.at[kv, half], p_s.at[kv, half], p_r.at[kv, half], sx)

    def join(half):
        cols = slice(half * 2 * HEAD, (half + 1) * 2 * HEAD)
        for kv in range(2):
            part_copy(kv, half).wait_recv()
            newkv[kv, :, cols] = (pacc[kv, :, cols] + precv[kv, half].astype(F32)).astype(BF16)

    def finish(n):
        row = lax.broadcasted_iota(jnp.int32, (QROWS, 2 * ROWS), 0) % ROWS + s * ROWS
        col = lax.broadcasted_iota(jnp.int32, (QROWS, 2 * ROWS), 1)
        shut = jnp.where(col <= row, 0.0, NEG)
        score, value = prompt_piece(n, 4, z_from(0, 4))
        new_score = dot_t(qs[n], newkv[0, :, lanes[n]]) * SCALE + shut
        _, den, out = update(n, [score, new_score], [value, newkv[1, :, lanes[n]]], False)
        out = out / jnp.sum(den, axis=1, keepdims=True)
        for g in range(GROUP):
            cols = pl.ds(pl.multiple_of((heads[n] * GROUP + g) * HEAD, HEAD), HEAD)
            o_ref[:, cols] = out[g * ROWS : (g + 1) * ROWS].astype(BF16)

    events, tasks = [], []

    def event(time, fn, *args):
        events.append((time, len(events), fn, args))

    def task(time, length, fn, *args):
        tasks.append((time, length, fn, args))

    for stream in range(NX):
        for i in range(2):
            event(XTIME[stream] + 0.5 * i, z_start, stream, i)
            for way in range(2):
                for d in range(1, z_reach(way, i) + 1):
                    event(ZTIME[stream] + ZHOP[stream] * (d - 1) + 0.5 * i, z_event, stream, way, i, d)
    event(0.6, split_x)
    event(XTIME[2] + 0.6, send_x, 0, 1)
    event(XTIME[3] + 0.6, send_x, 1, 4)
    full = [ZTIME[3] + ZHOP[3] * (d - 1) + 0.6 for d in range(5)]
    event(full[3] + 2.0, take_event, 0)
    event(full[3] + 2.5, take_event, 1)
    for wave, n in zip(WAVES, WAVE_HEADS):
        event(wave + 2.0, y_start, n)
        for way in range(2):
            for d in range(1, REACH[way][n % 2] + 1):
                event(wave + 2.5 + HOP * d, y_event, way, n, d)
    for p in range(4):
        for m in range(2):
            ready = max(11.0 + 3.5 * p, WAVES[3] + 2.6 + HOP * (p + 1) + 2.5 * m)
            task(ready, 0.7, project, m, p)
    task(ready + 6.0, 0.5, join, 0)
    task(9.0, 0.0, wait_own)
    for d in range(4):
        ready = 9.0 if d == 0 else full[d]
        for n in range(KV_HEADS):
            if d and n == KV_HEADS - 1:
                ready += 2.6
                task(ready, 0.0, wait_neighbour, d)
            task(ready, 0.7 if d else 0.4, attend, n, d)
    tasks.sort(key=lambda e: (e[2] not in (project, join), e[0]))
    events.sort(key=lambda e: e[:2])
    now = 0.0
    while events or tasks:
        ready = [t for t in tasks if t[0] <= now]
        if events and events[0][0] <= now:
            _, _, fn, args = events.pop(0)
            fn(*args)
            now += 0.1
        elif ready:
            tasks.remove(ready[0])
            _, length, fn, args = ready[0]
            fn(*args)
            now += length
        else:
            now = min([e[0] for e in events[:1]] + [t[0] for t in tasks])
    for n in range(KV_HEADS):
        if n == 1:
            join(1)
        if n == KV_HEADS - 1:
            wait_neighbour(4)
        finish(n)

    for queue in flying.values():
        for copy in queue:
            copy.wait_send()
    for _, _, copy in phase:
        copy.wait_send()

    @pl.when(c == s)
    def _():
        for g in range(2 * KV_HEADS):
            sib_copy(g, y).wait_send()


def attention(resp_x, queries, key_weight, value_weight, prompt_key, prompt_values, prompt_len):
    dma = pltpu.SemaphoreType.DMA
    any_space = pl.BlockSpec(memory_space=pl.ANY)
    return pl.pallas_call(
        kernel,
        out_shape=jax.ShapeDtypeStruct((ROWS, KV_HEADS * GROUP * HEAD), BF16),
        in_specs=[any_space] * 6 + [pl.BlockSpec(memory_space=pltpu.SMEM)],
        out_specs=pl.BlockSpec(memory_space=pltpu.VMEM),
        scratch_shapes=[
            pltpu.VMEM((2, NZ, BLOCK, KV_HEADS * HEAD), BF16),
            pltpu.VMEM((2, 4, XCOLS, 4 * WCOLS), BF16),
            pltpu.VMEM((ROWS, 8 * XCOLS), BF16),
            pltpu.VMEM((4, ROWS, XCOLS), BF16),
            pltpu.VMEM((4, 2 * ROWS, XCOLS), BF16),
            pltpu.VMEM((KV_HEADS, QROWS, HEAD), BF16),
            pltpu.VMEM((2, 2 * ROWS, 4 * WCOLS), F32),
            pltpu.VMEM((2, 2, 2 * ROWS, 2 * WCOLS), BF16),
            pltpu.VMEM((2, 2, 2 * ROWS, 2 * WCOLS), BF16),
            pltpu.VMEM((2, 2 * ROWS, 4 * WCOLS), BF16),
            pltpu.VMEM((KV_HEADS, QROWS, HEAD), F32),
            pltpu.VMEM((KV_HEADS, QROWS, HEAD), F32),
            pltpu.VMEM((KV_HEADS, QROWS, HEAD), F32),
            dma((2,)), dma((KV_HEADS * GROUP,)), dma((1,)), dma((8,)),
            dma((2, 3)), dma((2, 3)),
            dma((4, 2, 2, 5)), dma((4, 2, 2, 5)),
            dma((2,)), dma((2,)),
            dma((2, 2, 5)), dma((2, 2, 5)),
            dma((2, 4, 5)), dma((2, 4, 5)),
            dma((2, 4, 8)), dma((2, 4, 8)),
            dma((4,)), dma((4,)),
            dma((2, 2)), dma((2, 2)),
        ],
        compiler_params=pltpu.CompilerParams(
            collective_id=0, has_side_effects=True, vmem_limit_bytes=56 << 20
        ),
        cost_estimate=pl.CostEstimate(flops=4_400_000_000, bytes_accessed=8_000_000, transcendentals=6_000_000),
    )(resp_x, queries, key_weight, value_weight, prompt_key, prompt_values, prompt_len)


def local(
    resp_x, queries, key_weight, value_weight, prompt_key, cached_prompt_values, lengths, prompt_len
):
    mixed = attention(
        resp_x, queries, key_weight, value_weight, prompt_key, cached_prompt_values, prompt_len
    )
    row = lax.axis_index("seq") * ROWS + jnp.arange(ROWS, dtype=jnp.int32)
    live = (row < lengths[0, 0])[:, None]
    return jnp.where(live, mixed, jnp.zeros((), BF16))[None, None]


def solution(mesh):
    return jax.shard_map(
        local,
        mesh=mesh,
        in_specs=(
            P("blk", "pair", "seq", None),
            P("blk", "pair", "seq", None),
            P("blk", None),
            P("blk", None),
            P("blk", ("pair", "seq"), None),
            P("blk", ("pair", "seq"), None),
            P("blk", "pair"),
            P("blk"),
        ),
        out_specs=P("blk", "pair", "seq", None),
        check_vma=False,
    )
```
